128 devices in a mesh: front: 8 (over x, core), row: 4 (over z), col: 4 (over y).
Axes of the slice: x: 4, y: 4, z: 4, core: 2. Of those that a mesh axis runs over, the one named last changes fastest.
Arguments:
- parent_front: float32 [8, 4096, 4096], P('front', 'row', 'col'), may hold values from -6 to 6
- child_tiles: float32 [4096, 256, 256], P(('front', 'row', 'col')), may hold values from -6 to 6
- destination: int32 [4096, 1], P(('front', 'row', 'col')), may hold values from 0 to 31; in each aligned block of 32 rows (0 to 31, 32 to 63, ...) at most 2 rows name the same one
- row_map: int32 [4096, 256], P(('front', 'row', 'col')), may hold values from 0 to 1023, as said below
- col_map: int32 [4096, 256], P(('front', 'row', 'col')), may hold values from 0 to 1023, as said below
- pivot_inverse: float32 [8, 2, 256, 256], P('front')
Outputs:
- factored: float32 [8, 4096, 4096], P('front', 'row', 'col')
The draws below stay inside these ranges and needn't reach their ends.
Inputs may be any that keep to these rules, and one draw needn't show every extreme that they name: `destination`: in each device's block of 32 rows no value appears more than 2 times. `row_map`: each row's entries are distinct and lie in one aligned block of 256. `col_map`: each row's entries are distinct and lie in one aligned block of 256.
All inputs are finite; a program needn't handle non-finite values.
Results may differ from the reference program's by a relative error of at most 0.00014.
Values sent between devices are 32-bit elements; how exact they have to be, the bound alone decides.
No kernel may reach another device: no remote copies, remote signals or barrier semaphores. Data moves between devices by JAX's collectives and lax.ppermute only.
A program may use at most 128 MiB of HBM per device.

```python
import math
import jax
import jax.numpy as jnp
import numpy as np
from jax import lax

F = 4096
TILE = 256
PANELS = 2
KDEV = 32
FRONTS = 8
NDEST = 32
CAP = 2
TILES = 4096
BLOCK = 1024
BLOCKC = 1024
N_ROW = 4
N_COL = 4


def shuffle(single_key):
    return jax.random.permutation(single_key, TILE)


def local_map(key, width):
    first, second = jax.random.split(key)
    blocks = width // TILE
    starts = jax.random.randint(first, (TILES,), 0, blocks)
    starts = jnp.where(jnp.arange(TILES) == 0, blocks - 1, starts)
    orders = jax.vmap(shuffle)(jax.random.split(second, TILES))
    return (starts[:, None] * TILE + orders).astype(jnp.int32)


def draw_row_map(key, part):
    key = jax.random.fold_in(key, 11)
    return local_map(key, BLOCK)


def draw_col_map(key, part):
    key = jax.random.fold_in(key, 13)
    return local_map(key, BLOCKC)


def draw_pivot_inverse(key, part):
    key = jax.random.fold_in(key, 17)
    shape = (FRONTS, PANELS, TILE, TILE)
    noise = jax.random.normal(key, shape, jnp.float32)
    identity = jnp.eye(TILE, dtype=jnp.float32)
    return identity / math.sqrt(TILE) + noise * (0.3 / TILE)


def levels(key, dims, cuts, least, largest):
    def one(position, blocks):
        heights = jax.random.uniform(jax.random.fold_in(jax.random.fold_in(key, 6), position), (blocks,), jnp.float32, least / len(cuts), largest / len(cuts))
        return jnp.repeat(jnp.exp(heights), dims[position] // blocks).reshape((-1,) + (1,) * (len(dims) - position - 1))

    factor_of = one(*cuts[0])
    for cut in cuts[1:]:
        factor_of = factor_of * one(*cut)
    return factor_of


def deal_out(own_key, own, number, rows, amount, top, limit, lean):
    order = jax.random.permutation(own_key, amount)
    packed, common = portions_of(amount, rows * top, limit, lean, True), portions_of(amount, rows * top, limit, lean, False)
    places = jnp.arange(amount)

    def named(tallies, turn):
        used = int((tallies > 0).sum())
        fixed = max(1, used // 4)
        moved = fixed + (places - fixed + turn * (used - fixed)) % max(1, amount - fixed)
        return jnp.zeros((amount,), jnp.int32).at[order[jnp.where(places < fixed, places, moved)]].set(jnp.asarray(tallies, jnp.int32))

    tallies = jnp.where(number % 4 == 0, named(packed, number // 4), named(common, number - number // 4 - 1))
    mixed = jax.random.permutation(jax.random.fold_in(own, 3), amount)
    donor, receiver = mixed[0:amount // 2 * 2:2], mixed[1:amount // 2 * 2:2]
    margin = jnp.minimum(tallies[donor] - 1, limit - tallies[receiver]) // 2
    margin = jnp.where((donor == order[0]) | (receiver == order[0]) | (tallies[receiver] == 0), 0, jnp.maximum(margin, 0))
    moved = jax.random.randint(jax.random.fold_in(own, 4), (amount // 2,), 0, 1 << 20) % (margin + 1)
    tallies = tallies.at[donor].add(-moved).at[receiver].add(moved)
    labels = jnp.searchsorted(jnp.cumsum(tallies), jnp.arange(rows * top), side="right").astype(jnp.int32)
    grid = labels.reshape(top, rows).T
    grid = grid[jax.random.permutation(jax.random.fold_in(own, 1), rows)]
    turn = jax.random.randint(jax.random.fold_in(own, 2), (rows, 1), 0, top)
    return jnp.take_along_axis(grid, (jnp.arange(top)[None, :] + turn) % top, axis=1)


def portions_of(count, total, limit, slope, full):
    loads = [(1 << 20) // math.isqrt(rank ** slope) + 1 for rank in range(1, count + 1)]
    largest = limit if full else min(limit, max(-(-total // count), total * loads[0] // sum(loads)))
    least = 1 if total - largest >= count - 1 else 0
    holding, surplus = [largest] + [least] * (count - 1), total - largest - least * (count - 1)
    while surplus > 0:
        movable = [i for i in range(1, count) if holding[i] < largest] or [i for i in range(1, count) if holding[i] < limit]
        pool, remaining = sum([loads[i] for i in movable]), surplus
        for i in movable:
            more = min(limit - holding[i], max(1, remaining * loads[i] // pool), surplus)
            holding[i] = holding[i] + more
            surplus = surplus - more
    return np.array(holding)


def normal_values(stream_key, shape, scale, reach, pieces=(), kind=jnp.bfloat16):
    values = scale * jax.random.normal(stream_key, shape, jnp.float32)
    if pieces:
        values = values * levels(stream_key, shape, pieces, -0.22, 0.18)
    return jnp.clip(values, -reach, reach).astype(kind)


def setup_inputs(seed: int = 0) -> dict:
    arg_keys = jax.random.split(jax.random.key(seed), 7)
    parent_front = normal_values(arg_keys[0], (FRONTS, F, F), 1.0, 6.0, ((0, 8), (1, 4), (2, 4)), jnp.float32)
    child_tiles = normal_values(arg_keys[1], (TILES, TILE, TILE), 1.0, 6.0, ((0, 128),), jnp.float32)
    destination_keys = jax.random.split(jax.random.fold_in(arg_keys[2], 1), TILES // KDEV)
    destination_turns = jax.random.permutation(jax.random.fold_in(arg_keys[2], 3), TILES // KDEV)
    destination = jax.vmap(lambda own, number: deal_out(jax.random.fold_in(arg_keys[2], 2), own, number, KDEV, NDEST, 1, CAP, 2))(destination_keys, destination_turns).reshape((TILES, 1))
    row_map = draw_row_map(jax.random.fold_in(arg_keys[6], 71), 0)
    col_map = draw_col_map(jax.random.fold_in(arg_keys[6], 71), 0)
    pivot_inverse = draw_pivot_inverse(jax.random.fold_in(arg_keys[6], 71), 0)
    return {"parent_front": parent_front, "child_tiles": child_tiles, "destination": destination, "row_map": row_map, "col_map": col_map, "pivot_inverse": pivot_inverse}


def eliminate(matrix, inverses):
    index = jnp.arange(F)
    for panel in range(PANELS):
        start = panel * TILE
        stop = start + TILE
        factor = jnp.dot(matrix[:, start:stop], inverses[panel], precision=lax.Precision.HIGHEST, preferred_element_type=jnp.float32)
        update = jnp.dot(factor, matrix[start:stop, :], precision=lax.Precision.HIGHEST, preferred_element_type=jnp.float32)
        trailing = (index >= stop)[:, None] & (index >= stop)[None, :]
        matrix = jnp.where(trailing, matrix - update, matrix)
        below = (index >= stop)[:, None]
        matrix = matrix.at[:, start:stop].set(jnp.where(below, factor, matrix[:, start:stop]))
    return matrix


def reference(parent_front, child_tiles, destination, row_map, col_map, pivot_inverse):
    target = destination[:, 0].astype(jnp.int32)
    fronts_of = (target // N_ROW).astype(jnp.int32)
    row_blocks = (target % N_ROW).astype(jnp.int32)
    col_blocks = ((jnp.arange(TILES) // KDEV) % N_COL).astype(jnp.int32)

    def add_tile(carry, items):
        values, front_id, row_block, col_block, rows_in, cols_in = items
        rows = row_block * BLOCK + rows_in
        columns = col_block * BLOCKC + cols_in
        carry = carry.at[front_id, rows[:, None], columns[None, :]].add(values)
        return carry, None

    assembled, _ = lax.scan(add_tile, parent_front, (child_tiles, fronts_of, row_blocks, col_blocks, row_map.astype(jnp.int32), col_map.astype(jnp.int32)))
    return lax.map(lambda pair: eliminate(pair[0], pair[1]), (assembled, pivot_inverse))
```

```python
import jax
import jax.numpy as jnp
from jax import lax
from jax.experimental import pallas as pl
from jax.experimental.pallas import tpu as pltpu
from jax.sharding import PartitionSpec as P

PLANE = ("front", "row")
W = 256
SUBS = 4
FULL = SUBS * W
HALF = 2 * W
STRIP = 8
NJ = 32
RING = 4
ANY = pl.BlockSpec(memory_space=pl.ANY)
VMEM = pl.BlockSpec(memory_space=pltpu.VMEM)
SMEM = pl.BlockSpec(memory_space=pltpu.SMEM)
DMA = pltpu.SemaphoreType.DMA


def f32(*shape):
    return jax.ShapeDtypeStruct(shape, jnp.float32)


def space(*shape, dtype=jnp.float32):
    return pltpu.VMEM(shape, dtype)


def params(flops, moved):
    return {
        "compiler_params": pltpu.CompilerParams(vmem_limit_bytes=62 * 1024 * 1024),
        "cost_estimate": pl.CostEstimate(flops=flops, bytes_accessed=moved, transcendentals=0),
    }


def split(value):
    high = value.astype(jnp.bfloat16)
    low = (value - high.astype(jnp.float32)).astype(jnp.bfloat16)
    return high, low


def dot(a, b):
    return jnp.dot(a, b, preferred_element_type=jnp.float32)


def dot3(a, b):
    ah, al = a
    bh, bl = b
    return dot(ah, bh) + (dot(ah, bl) + dot(al, bh))


def place_of(row, col):
    least = jnp.minimum(row, col)
    first = jnp.where(col == 0, row, 3 + col)
    second = jnp.where(col == 1, 6 + row, 8 + col)
    rest = 12 + (row - 2) * 2 + (col - 2)
    return jnp.where(least == 0, first, jnp.where(least == 1, second, rest))


PLACE = {}
for _r in range(SUBS):
    for _c in range(SUBS):
        PLACE[_r, _c] = (
            (_r if _c == 0 else 3 + _c)
            if min(_r, _c) == 0
            else (6 + _r if _c == 1 else 8 + _c)
            if min(_r, _c) == 1
            else 12 + (_r - 2) * 2 + _c - 2
        )


def permute_kernel(dest_ref, rows_ref, cols_ref, tiles_hbm, out_hbm, tiles, out, in_sems, out_sems):
    count = tiles.shape[0]
    groups = in_sems.shape[0]
    step = count // groups
    index = lax.broadcasted_iota(jnp.int32, (W, W), 0)
    contract = (((1,), (1,)), ((), ()))

    def load(g):
        at = pl.ds(g * step, step)
        return pltpu.make_async_copy(tiles_hbm.at[at], tiles.at[at], in_sems.at[g])

    def store(k, first, last):
        at = pl.ds(first, last - first)
        return pltpu.make_async_copy(out.at[:, at], out_hbm.at[:, at], out_sems.at[k])

    def work(g, carry):
        load(g).wait()
        for k in range(step):
            i = g * step + k
            rows = rows_ref[pl.ds(i, 1), :] & (W - 1)
            cols = cols_ref[pl.ds(i, 1), :] & (W - 1)
            row_hot = (index == rows).astype(jnp.float32).astype(jnp.bfloat16)
            col_hot = (index == cols).astype(jnp.float32).astype(jnp.bfloat16)
            high, low = split(tiles[i])
            high = lax.dot_general(high, col_hot, contract, preferred_element_type=jnp.float32)
            low = lax.dot_general(low, col_hot, contract, preferred_element_type=jnp.float32)
            moved = dot(row_hot, high.astype(jnp.bfloat16)) + dot(
                row_hot, low.astype(jnp.bfloat16)
            )
            out[:, i] = moved.reshape(NJ, STRIP, W)
        return carry

    for g in range(groups):
        load(g).start()
    place = place_of(rows_ref[:, :1] // W, cols_ref[:, :1] // W)
    place = place.astype(jnp.float32)
    same = lax.broadcasted_iota(jnp.int32, (count, W), 0) == lax.broadcasted_iota(
        jnp.int32, (count, W), 1
    )
    line = jnp.sum(jnp.where(same, place, 0.0), axis=0, keepdims=True)
    out[:, count] = jnp.broadcast_to(line[None], (NJ, STRIP, W))
    line = line[:, :count] + (dest_ref[...] * (SUBS * SUBS)).astype(jnp.float32)
    out[:, count, :, :count] = jnp.broadcast_to(line[None], (NJ, STRIP, count))
    half = groups // 2
    lax.fori_loop(0, half, work, 0)
    store(0, 0, half * step).start()
    lax.fori_loop(half, groups, work, 0)
    store(1, half * step, count + 1).start()
    store(0, 0, half * step).wait()
    store(1, half * step, count + 1).wait()


def permute_tiles(child_tiles, destination, row_map, col_map):
    count = child_tiles.shape[0]
    groups = 4
    return pl.pallas_call(
        permute_kernel,
        in_specs=[VMEM, VMEM, VMEM, ANY],
        out_specs=ANY,
        out_shape=f32(NJ, count + 1, STRIP, W),
        scratch_shapes=[
            space(count, W, W),
            space(NJ, count + 1, STRIP, W),
            DMA((groups,)),
            DMA((2,)),
        ],
        name="permute",
        **params(8 * count * W**3, 8 * count * W * W),
    )(destination.reshape(1, count), row_map, col_map, child_tiles)


def reduce_kernel(strips_hbm, out_hbm, strips, sums, lines, codes_vmem, codes, sems, sem):
    count = strips.shape[1]
    groups = sems.shape[0]
    step = NJ // groups

    def load(g):
        at = pl.ds(g * step, step)
        return pltpu.make_async_copy(
            strips_hbm.at[at, pl.ds(0, count)], strips.at[at], sems.at[g]
        )

    line_copy = pltpu.make_async_copy(
        strips_hbm.at[:, count, :, pl.ds(0, 128)], lines, sem.at[0]
    )
    line_copy.start()
    for g in range(groups):
        load(g).start()
    sums[...] = jnp.zeros_like(sums)
    line_copy.wait()
    codes_vmem[...] = lines[:, 0].astype(jnp.int32)
    code_copy = pltpu.make_async_copy(codes_vmem, codes, sem.at[1])
    code_copy.start()
    code_copy.wait()
    for g in range(groups):
        load(g).wait()

        def add(i, carry):
            source = g * step + i // (count // 8)
            tile = i % (count // 8) * 8
            for k in range(8):
                code = codes[source, tile + k]
                sums[code] = sums[code] + strips[source, tile + k]
            return carry

        lax.fori_loop(0, step * (count // 8), add, 0, unroll=2)
    done = pltpu.make_async_copy(sums, out_hbm, sem.at[2])
    done.start()
    done.wait()


def reduce_strips(strips, slots):
    count = strips.shape[1] - 1
    groups = 8
    return pl.pallas_call(
        reduce_kernel,
        in_specs=[ANY],
        out_specs=ANY,
        out_shape=f32(slots, STRIP, W),
        scratch_shapes=[
            space(NJ, count, STRIP, W),
            space(slots, STRIP, W),
            space(NJ, STRIP, 128),
            space(NJ, 128, dtype=jnp.int32),
            pltpu.SMEM((NJ, 128), jnp.int32),
            DMA((groups,)),
            DMA((3,)),
        ],
        name="reduce",
        **params(NJ * count * STRIP * W, 4 * (NJ * count + slots) * STRIP * W),
    )(strips)


def first_kernel(parent_hbm, got_hbm, inv_ref, *refs):
    outs, (column, pivot, got, left, right, sems, out_sems) = refs[:4], refs[4:]
    copies = [
        pltpu.make_async_copy(got_hbm.at[:, pl.ds(0, 7)], got, sems.at[0]),
        pltpu.make_async_copy(parent_hbm.at[:, pl.ds(0, W)], column, sems.at[1]),
        pltpu.make_async_copy(parent_hbm.at[pl.ds(0, W)], pivot, sems.at[2]),
    ]
    for copy in copies:
        copy.start()
    inv = split(inv_ref[0])
    for copy in copies:
        copy.wait()
    stores = halves(outs, left, right, out_sems)
    for k in range(SUBS):
        at = slice(k * W, (k + 1) * W)
        values = column[at] + got[:, PLACE[k, 0]].reshape(W, W)
        left[at] = dot3(split(values), inv)
        right[:, at] = pivot[:, at] + got[:, PLACE[0, k]].reshape(W, W)
        if k % 2:
            stores[k // 2].start()
            stores[2 + k // 2].start()
    for store in stores:
        store.wait()


def halves(outs, left, right, sems):
    parts = [
        left.at[pl.ds(0, HALF)],
        left.at[pl.ds(HALF, HALF)],
        right.at[:, pl.ds(0, HALF)],
        right.at[:, pl.ds(HALF, HALF)],
    ]
    return [pltpu.make_async_copy(parts[k], outs[k], sems.at[k]) for k in range(4)]


HALVES = [f32(HALF, W), f32(HALF, W), f32(W, HALF), f32(W, HALF)]


def first_panel(parent, got, inverses):
    return pl.pallas_call(
        first_kernel,
        in_specs=[ANY, ANY, VMEM],
        out_specs=[ANY] * 4,
        out_shape=HALVES,
        scratch_shapes=[
            space(FULL, W),
            space(W, FULL),
            space(NJ, 7, STRIP, W),
            space(FULL, W),
            space(W, FULL),
            DMA((3,)),
            DMA((4,)),
        ],
        name="first_panel",
        **params(6 * FULL * W * W, 24 * FULL * W),
    )(parent, got, inverses)


def assemble_kernel(parent_ref, got_ref, all_ref):
    step = pl.program_id(0)
    for r in range(SUBS):

        @pl.when(step == r)
        def _():
            for c in range(SUBS):
                at = slice(c * W, (c + 1) * W)
                all_ref[:, at] = parent_ref[:, at] + got_ref[:, PLACE[r, c]].reshape(W, W)


def assemble(parent, got):
    return pl.pallas_call(
        assemble_kernel,
        grid=(SUBS,),
        in_specs=[pl.BlockSpec((W, FULL), lambda i: (i, 0)), VMEM],
        out_specs=pl.BlockSpec((W, FULL), lambda i: (i, 0)),
        out_shape=f32(FULL, FULL),
        name="assemble",
        **params(FULL * FULL, 12 * FULL * FULL),
    )(parent, got)


def fetch(index, near, parts, target, sem):
    own, first, second = parts

    @pl.when(index == 0)
    def _():
        pltpu.make_async_copy(own, target, sem).start()

    @pl.when(index == near)
    def _():
        pltpu.make_async_copy(first, target, sem).start()

    @pl.when((index != 0) & (index != near))
    def _():
        pltpu.make_async_copy(second, target, sem).start()

    return pltpu.make_async_copy(own, target, sem)


def fetch_all(place_ref, pieces, left, right, sems):
    row, col = place_ref[0], place_ref[1]
    return [
        fetch(col, 1, pieces[0:3], left.at[pl.ds(0, HALF)], sems.at[0]),
        fetch(col, 3, pieces[3:6], left.at[pl.ds(HALF, HALF)], sems.at[1]),
        fetch(row, 1, pieces[6:9], right.at[:, pl.ds(0, HALF)], sems.at[2]),
        fetch(row, 3, pieces[9:12], right.at[:, pl.ds(HALF, HALF)], sems.at[3]),
    ]


def second_kernel(place_ref, *refs):
    pieces = refs[:12]
    matrix, inv_ref, *outs = refs[12:18]
    left, right, column, pivot, sems, out_sems = refs[18:]
    row, col = place_ref[0], place_ref[1]
    copies = fetch_all(place_ref, pieces, left, right, sems)
    copies.append(pltpu.make_async_copy(matrix.at[:, pl.ds(W, W)], column, sems.at[4]))
    copies.append(pltpu.make_async_copy(matrix.at[pl.ds(W, W)], pivot, sems.at[5]))
    for copy in copies[4:]:
        copy.start()
    for copy in copies:
        copy.wait()
    stores = halves(outs, column, pivot, out_sems)

    @pl.when(col == 0)
    def _():
        inv = split(inv_ref[1])
        corner = split(right[:, W:HALF])
        for k in range(SUBS):
            at = slice(k * W, (k + 1) * W)
            reduced = column[at] - dot3(split(left[at]), corner)
            column[at] = dot3(split(reduced), inv)
            if k % 2:
                stores[k // 2].start()

    @pl.when(row == 0)
    def _():
        below = split(left[W:HALF])
        for k in range(SUBS):
            at = slice(k * W, (k + 1) * W)
            pivot[:, at] = pivot[:, at] - dot3(below, split(right[:, at]))
            if k % 2:
                stores[2 + k // 2].start()

    @pl.when(col == 0)
    def _():
        stores[0].wait()
        stores[1].wait()

    @pl.when(row == 0)
    def _():
        stores[2].wait()
        stores[3].wait()


def second_panel(place, pieces, matrix, inverses):
    return pl.pallas_call(
        second_kernel,
        in_specs=[SMEM] + [ANY] * 13 + [VMEM],
        out_specs=[ANY] * 4,
        out_shape=HALVES,
        scratch_shapes=[
            space(FULL, W),
            space(W, FULL),
            space(FULL, W),
            space(W, FULL),
            DMA((6,)),
            DMA((4,)),
        ],
        name="second_panel",
        **params(18 * FULL * W * W, 32 * FULL * W),
    )(place, *pieces, matrix, inverses)


def update_kernel(panel, place_ref, *refs):
    pieces = refs[:12]
    matrix, out_hbm, left, right, high, low, held, sems, in_sems, out_sems = refs[12:]
    row, col = place_ref[0], place_ref[1]

    def copy(k, source, target, sem):
        at = pl.ds(k * W, W)
        return pltpu.make_async_copy(source.at[at], target.at[at], sem.at[k])

    copies = fetch_all(place_ref, pieces, left, right, sems)
    for k in range(SUBS):
        copy(k, matrix, held, in_sems).start()
    for c in (2, 3, 0, 1):
        copies[c].wait()
    values = split(right[...])
    high[...] = values[0]
    low[...] = values[1]
    for k in range(SUBS):
        at = slice(k * W, (k + 1) * W)
        copy(k, matrix, held, in_sems).wait()
        trailing = row * SUBS + k > panel
        values = left[at]
        factor = split(values)

        @pl.when(trailing & (col == 0))
        def _():
            edge = (panel + 1) * W
            held[at, panel * W : edge] = values
            held[at, edge:] = held[at, edge:] - dot3(factor, (high[:, edge:], low[:, edge:]))

        @pl.when(trailing & (col != 0))
        def _():
            held[at] = held[at] - dot3(factor, (high[...], low[...]))

        copy(k, held, out_hbm, out_sems).start()
    for k in range(SUBS):
        copy(k, held, out_hbm, out_sems).wait()


def update(panel, place, matrix, pieces):
    return pl.pallas_call(
        lambda *refs: update_kernel(panel, *refs),
        in_specs=[SMEM] + [ANY] * 13,
        out_specs=ANY,
        out_shape=f32(FULL, FULL),
        scratch_shapes=[
            space(FULL, W),
            space(W, FULL),
            space(W, FULL, dtype=jnp.bfloat16),
            space(W, FULL, dtype=jnp.bfloat16),
            space(FULL, FULL),
            DMA((4,)),
            DMA((SUBS,)),
            DMA((SUBS,)),
        ],
        name="update",
        **params(6 * FULL * FULL * W, 10 * FULL * FULL),
    )(place, *pieces, matrix)


def exchange(value):
    return lax.all_to_all(value, PLANE, split_axis=0, concat_axis=0, tiled=True)


def broadcast(halves, beside):
    la, lb, ra, rb = halves
    row, col = lax.axis_index("row"), lax.axis_index("col")
    la1 = lax.ppermute(la, "col", [(0, 1)])
    ra1 = lax.ppermute(ra, "row", [(0, 1)])
    lb1 = lax.ppermute(lb, "col", [(0, 3)])
    rb1 = lax.ppermute(rb, "row", [(0, 3)])
    la1, lb1, ra1, rb1, beside = lax.optimization_barrier((la1, lb1, ra1, rb1, beside))
    la2 = lax.ppermute(jnp.where(col == 1, la1, la), "col", [(0, 3), (1, 2)])
    ra2 = lax.ppermute(jnp.where(row == 1, ra1, ra), "row", [(0, 3), (1, 2)])
    lb2 = lax.ppermute(jnp.where(col == 3, lb1, lb), "col", [(0, 1), (3, 2)])
    rb2 = lax.ppermute(jnp.where(row == 3, rb1, rb), "row", [(0, 1), (3, 2)])
    return (la, la1, la2, lb, lb1, lb2, ra, ra1, ra2, rb, rb1, rb2), beside


def per_device(parent_front, child_tiles, destination, row_map, col_map, pivot_inverse):
    parent = parent_front[0]
    inverses = pivot_inverse[0]
    place = jnp.stack([lax.axis_index("row"), lax.axis_index("col")]).astype(jnp.int32)
    subs = SUBS * SUBS
    strips = exchange(permute_tiles(child_tiles, destination, row_map, col_map))
    got = exchange(reduce_strips(strips, NJ * subs).reshape(NJ, subs, STRIP, W))
    pieces, matrix = broadcast(first_panel(parent, got, inverses), assemble(parent, got))
    second = second_panel(place, pieces, matrix, inverses)
    later, matrix = broadcast(second, update(0, place, matrix, pieces))
    return update(1, place, matrix, later)[None]


def solution(mesh):
    in_specs = (
        P("front", "row", "col"),
        P(("front", "row", "col"), None, None),
        P(("front", "row", "col"), None),
        P(("front", "row", "col"), None),
        P(("front", "row", "col"), None),
        P("front", None, None, None),
    )
    out_specs = P("front", "row", "col")
    return jax.shard_map(
        per_device, mesh=mesh, in_specs=in_specs, out_specs=out_specs, check_vma=False
    )
```

```python
import jax
import jax.numpy as jnp
from jax import lax
from jax.experimental import pallas as pl
from jax.experimental.pallas import tpu as pltpu
from jax.sharding import PartitionSpec as P

PLANE = ("front", "row")
W = 256
SUBS = 4
FULL = SUBS * W
HALF = 2 * W
STRIP = 8
LANES = 128
NJ = 32
RING = 4
HBM = pl.BlockSpec(memory_space=pltpu.HBM)
VMEM = pl.BlockSpec(memory_space=pltpu.VMEM)
DMA = pltpu.SemaphoreType.DMA


def f32(*shape):
    return jax.ShapeDtypeStruct(shape, jnp.float32)


def space(*shape, dtype=jnp.float32):
    return pltpu.VMEM(shape, dtype)


def params(flops, moved, mib=18):
    return {
        "compiler_params": pltpu.CompilerParams(vmem_limit_bytes=mib * 1024 * 1024),
        "cost_estimate": pl.CostEstimate(flops=flops, bytes_accessed=moved, transcendentals=0),
    }


def split(value):
    high = value.astype(jnp.bfloat16)
    low = (value - high.astype(jnp.float32)).astype(jnp.bfloat16)
    return high, low


def dot(a, b):
    return jnp.dot(a, b, preferred_element_type=jnp.float32)


def dot3(a, b):
    ah, al = a
    bh, bl = b
    return dot(ah, bh) + (dot(ah, bl) + dot(al, bh))


def place_of(row, col):
    least = jnp.minimum(row, col)
    first = jnp.where(col == 0, row, 3 + col)
    second = jnp.where(col == 1, 6 + row, 8 + col)
    rest = 12 + (row - 2) * 2 + (col - 2)
    return jnp.where(least == 0, first, jnp.where(least == 1, second, rest))


PLACE = {}
for _r in range(SUBS):
    for _c in range(SUBS):
        PLACE[_r, _c] = (
            (_r if _c == 0 else 3 + _c)
            if min(_r, _c) == 0
            else (6 + _r if _c == 1 else 8 + _c)
            if min(_r, _c) == 1
            else 12 + (_r - 2) * 2 + _c - 2
        )


GROUPS = (4, 12, 12, 4)


def permute_kernel(
    dest_hbm, rows_hbm, cols_hbm, tiles_hbm, out_hbm, dest, rows, cols, tiles, out, sems, out_sems
):
    count = tiles.shape[0]
    maps = [
        pltpu.make_async_copy(rows_hbm, rows, sems.at[0]),
        pltpu.make_async_copy(cols_hbm, cols, sems.at[1]),
        pltpu.make_async_copy(dest_hbm, dest, sems.at[2]),
    ]
    loads = []
    first = 0
    for k, size in enumerate(GROUPS):
        at = pl.ds(first, size)
        loads.append(pltpu.make_async_copy(tiles_hbm.at[at], tiles.at[at], sems.at[3 + k]))
        first += size
    for copy in maps + loads:
        copy.start()
    for copy in maps:
        copy.wait()

    place = place_of(rows[:, :1] // W, cols[:, :1] // W).astype(jnp.float32)
    same = lax.broadcasted_iota(jnp.int32, (count, LANES), 0) == lax.broadcasted_iota(
        jnp.int32, (count, LANES), 1
    )
    line = jnp.sum(jnp.where(same, place, 0.0), axis=0, keepdims=True)
    out[:, 2 * count] = jnp.broadcast_to(line[None], (NJ, STRIP, LANES))
    line = line[:, :count] + (dest[...] * (SUBS * SUBS)).astype(jnp.float32)
    out[:, 2 * count, :, :count] = jnp.broadcast_to(line[None], (NJ, STRIP, count))

    index = lax.broadcasted_iota(jnp.int32, (W, W), 0)
    stores = []
    contract = (((1,), (1,)), ((), ()))
    first = 0
    for load, size in zip(loads, GROUPS):
        load.wait()
        for i in range(first, first + size):
            row_hot = (index == (rows[i : i + 1] & (W - 1))).astype(jnp.float32)
            col_hot = (index == (cols[i : i + 1] & (W - 1))).astype(jnp.float32)
            row_hot = row_hot.astype(jnp.bfloat16)
            col_hot = col_hot.astype(jnp.bfloat16)
            high, low = split(tiles[i])
            high = dot(row_hot, high).astype(jnp.bfloat16)
            low = dot(row_hot, low).astype(jnp.bfloat16)
            moved = lax.dot_general(
                jnp.concatenate([high, low], axis=1),
                jnp.concatenate([col_hot, col_hot], axis=1),
                contract,
                preferred_element_type=jnp.float32,
            )
            out[:, 2 * i] = moved[:, :LANES].reshape(NJ, STRIP, LANES)
            out[:, 2 * i + 1] = moved[:, LANES:].reshape(NJ, STRIP, LANES)
        at = pl.ds(2 * first, 2 * size + (first + size == count))
        sem = out_sems.at[len(stores)]
        stores.append(pltpu.make_async_copy(out.at[:, at], out_hbm.at[:, at], sem))
        stores[-1].start()
        first += size
    for store in stores:
        store.wait()


def permute_tiles(child_tiles, destination, row_map, col_map):
    count = child_tiles.shape[0]
    return pl.pallas_call(
        permute_kernel,
        in_specs=[HBM] * 4,
        out_specs=HBM,
        out_shape=f32(NJ, 2 * count + 1, STRIP, LANES),
        scratch_shapes=[
            space(1, count, dtype=jnp.int32),
            space(count, W, dtype=jnp.int32),
            space(count, W, dtype=jnp.int32),
            space(count, W, W),
            space(NJ, 2 * count + 1, STRIP, LANES),
            DMA((3 + len(GROUPS),)),
            DMA((len(GROUPS),)),
        ],
        name="permute",
        **params(8 * count * W**3, 8 * count * W * W, 62),
    )(destination.reshape(1, count), row_map, col_map, child_tiles)


def reduce_kernel(strips, sums, codes_vmem, codes, sem):
    count = strips.shape[1] // 2
    codes_vmem[...] = strips[:, 2 * count, 0].astype(jnp.int32)
    copy = pltpu.make_async_copy(codes_vmem, codes, sem)
    copy.start()
    sums[...] = jnp.zeros_like(sums)
    copy.wait()

    def add(source, carry):
        for k in range(count):
            code = codes[source, k]
            sums[code] = sums[code] + strips[source, 2 * k : 2 * k + 2]
        return carry

    lax.fori_loop(0, NJ, add, 0)


def reduce_strips(strips, slots):
    count = strips.shape[1] // 2
    return pl.pallas_call(
        reduce_kernel,
        in_specs=[VMEM],
        out_specs=VMEM,
        out_shape=f32(slots, 2, STRIP, LANES),
        scratch_shapes=[
            space(NJ, LANES, dtype=jnp.int32),
            pltpu.SMEM((NJ, LANES), jnp.int32),
            DMA,
        ],
        name="reduce",
        **params(NJ * count * STRIP * W, 4 * (NJ * count + slots) * STRIP * W),
    )(strips)


def block(parent, got, r, c):
    place = PLACE[r, c]
    rows, cols = slice(r * W, (r + 1) * W), c * W
    left = parent[rows, cols : cols + LANES] + got[:, place, 0].reshape(W, LANES)
    right = parent[rows, cols + LANES : cols + W] + got[:, place, 1].reshape(W, LANES)
    return jnp.concatenate([left, right], axis=1)


def first_kernel(parent, got, inv_ref, la, lb, ra, rb):
    inv = split(inv_ref[0])
    for k in range(SUBS):
        half = slice(k % 2 * W, (k % 2 + 1) * W)
        (la, lb)[k // 2][half] = dot3(split(block(parent, got, k, 0)), inv)
        (ra, rb)[k // 2][:, half] = block(parent, got, 0, k)


HALVES = [f32(HALF, W), f32(HALF, W), f32(W, HALF), f32(W, HALF)]


def first_panel(parent, got, inverses):
    return pl.pallas_call(
        first_kernel,
        in_specs=[VMEM] * 3,
        out_specs=[VMEM] * 4,
        out_shape=HALVES,
        name="first_panel",
        **params(6 * FULL * W * W, 12 * FULL * W),
    )(parent, got, inverses)


def assemble_kernel(parent, got, matrix):
    for r in range(SUBS):
        for c in range(SUBS):
            rows, cols = slice(r * W, (r + 1) * W), slice(c * W, (c + 1) * W)
            matrix[rows, cols] = block(parent, got, r, c)


def assemble(parent, got):
    return pl.pallas_call(
        assemble_kernel,
        in_specs=[VMEM] * 2,
        out_specs=VMEM,
        out_shape=f32(FULL, FULL),
        name="assemble",
        **params(FULL * FULL, 12 * FULL * FULL),
    )(parent, got)


def choose(index, near, parts, target):
    own, first, second = parts

    @pl.when(index == 0)
    def _():
        target[...] = own[...]

    @pl.when(index == near)
    def _():
        target[...] = first[...]

    @pl.when((index != 0) & (index != near))
    def _():
        target[...] = second[...]


def choose_all(row, col, pieces, left, right):
    choose(col, 1, pieces[0:3], left.at[pl.ds(0, HALF)])
    choose(col, 3, pieces[3:6], left.at[pl.ds(HALF, HALF)])
    choose(row, 1, pieces[6:9], right.at[:, pl.ds(0, HALF)])
    choose(row, 3, pieces[9:12], right.at[:, pl.ds(HALF, HALF)])


def second_kernel(*refs):
    pieces = refs[:12]
    matrix, inv_ref, la, lb, ra, rb, left, right = refs[12:]
    row, col = lax.axis_index("row"), lax.axis_index("col")

    @pl.when((row == 0) | (col == 0))
    def _():
        choose_all(row, col, pieces, left, right)

    @pl.when(col == 0)
    def _():
        inv = split(inv_ref[1])
        corner = split(right[:, W:HALF])
        for k in range(SUBS):
            at = slice(k * W, (k + 1) * W)
            half = slice(k % 2 * W, (k % 2 + 1) * W)
            reduced = matrix[at, W:HALF] - dot3(split(left[at]), corner)
            (la, lb)[k // 2][half] = dot3(split(reduced), inv)

    @pl.when(row == 0)
    def _():
        below = split(left[W:HALF])
        for k in range(SUBS):
            at = slice(k * W, (k + 1) * W)
            half = slice(k % 2 * W, (k % 2 + 1) * W)
            (ra, rb)[k // 2][:, half] = matrix[W:HALF, at] - dot3(below, split(right[:, at]))


def second_panel(pieces, matrix, inverses):
    return pl.pallas_call(
        second_kernel,
        in_specs=[VMEM] * 14,
        out_specs=[VMEM] * 4,
        out_shape=HALVES,
        scratch_shapes=[space(FULL, W), space(W, FULL)],
        name="second_panel",
        **params(18 * FULL * W * W, 32 * FULL * W),
    )(*pieces, matrix, inverses)


def update_rows(panel, k, matrix, out, left, high, low):
    row, col = lax.axis_index("row"), lax.axis_index("col")
    at = slice(k * W, (k + 1) * W)
    edge = (panel + 1) * W
    trailing = row * SUBS + k > panel
    values = left[at]
    factor = split(values)

    @pl.when(jnp.logical_not(trailing))
    def _():
        out[at] = matrix[at]

    @pl.when(trailing & (col == 0))
    def _():
        if panel:
            out[at, : panel * W] = matrix[at, : panel * W]
        out[at, panel * W : edge] = values
        out[at, edge:] = matrix[at, edge:] - dot3(factor, (high[:, edge:], low[:, edge:]))

    @pl.when(trailing & (col != 0))
    def _():
        out[at] = matrix[at] - dot3(factor, (high[...], low[...]))


def prepare(pieces, left, right, high, low):
    choose_all(lax.axis_index("row"), lax.axis_index("col"), pieces, left, right)
    values = split(right[...])
    high[...] = values[0]
    low[...] = values[1]


def update_kernel(*refs):
    matrix, out, left, right, high, low = refs[12:]
    prepare(refs[:12], left, right, high, low)
    for k in range(SUBS):
        update_rows(0, k, matrix, out, left, high, low)


def finish_kernel(*refs):
    matrix, out_hbm, left, right, high, low, out, sems = refs[12:]
    prepare(refs[:12], left, right, high, low)
    stores = []
    for k in range(SUBS):
        update_rows(1, k, matrix, out, left, high, low)
        at = pl.ds(k * W, W)
        stores.append(pltpu.make_async_copy(out.at[at], out_hbm.at[at], sems.at[k]))
        stores[k].start()
    for store in stores:
        store.wait()


SCRATCH = [
    space(FULL, W),
    space(W, FULL),
    space(W, FULL, dtype=jnp.bfloat16),
    space(W, FULL, dtype=jnp.bfloat16),
]


def update(matrix, pieces):
    return pl.pallas_call(
        update_kernel,
        in_specs=[VMEM] * 13,
        out_specs=VMEM,
        out_shape=f32(FULL, FULL),
        scratch_shapes=SCRATCH,
        name="update",
        **params(6 * FULL * FULL * W, 10 * FULL * FULL),
    )(*pieces, matrix)


def finish(matrix, pieces):
    return pl.pallas_call(
        finish_kernel,
        in_specs=[VMEM] * 13,
        out_specs=HBM,
        out_shape=f32(FULL, FULL),
        scratch_shapes=SCRATCH + [space(FULL, FULL), DMA((SUBS,))],
        name="finish",
        **params(6 * FULL * FULL * W, 10 * FULL * FULL),
    )(*pieces, matrix)


def exchange(value):
    return lax.all_to_all(value, PLANE, split_axis=0, concat_axis=0, tiled=True)


RIGHT = [(k, (k + 1) % RING) for k in range(RING)]
LEFT = [(k, (k - 1) % RING) for k in range(RING)]
PAIRS = [(0, 1), (1, 0), (2, 3), (3, 2)]
CROSS = [(0, 3), (3, 0), (1, 2), (2, 1)]


def broadcast(halves, beside=()):
    la, lb, ra, rb = halves
    row, col = lax.axis_index("row"), lax.axis_index("col")
    la1 = lax.ppermute(la, "col", RIGHT)
    lb1 = lax.ppermute(lb, "col", LEFT)
    ra1 = lax.ppermute(ra, "row", RIGHT)
    rb1 = lax.ppermute(rb, "row", LEFT)
    la1, lb1 = lax.optimization_barrier((la1, lb1))
    ra1, rb1, beside = lax.optimization_barrier((ra1, rb1, beside))
    la2 = lax.ppermute(jnp.where(col == 1, la1, la), "col", CROSS)
    ra2 = lax.ppermute(jnp.where(row == 1, ra1, ra), "row", CROSS)
    lb2 = lax.ppermute(jnp.where(col == 3, lb1, lb), "col", PAIRS)
    rb2 = lax.ppermute(jnp.where(row == 3, rb1, rb), "row", PAIRS)
    return (la, la1, la2, lb, lb1, lb2, ra, ra1, ra2, rb, rb1, rb2), beside


def per_device(parent_front, child_tiles, destination, row_map, col_map, pivot_inverse):
    parent = parent_front[0]
    inverses = pivot_inverse[0]
    subs = SUBS * SUBS
    strips = exchange(permute_tiles(child_tiles, destination, row_map, col_map))
    got = exchange(reduce_strips(strips, NJ * subs).reshape(NJ, subs, 2, STRIP, LANES))
    pieces, matrix = broadcast(first_panel(parent, got, inverses), assemble(parent, got))
    second = second_panel(pieces, matrix, inverses)
    later, matrix = broadcast(second, update(matrix, pieces))
    return finish(matrix, later)[None]


def solution(mesh):
    in_specs = (
        P("front", "row", "col"),
        P(("front", "row", "col"), None, None),
        P(("front", "row", "col"), None),
        P(("front", "row", "col"), None),
        P(("front", "row", "col"), None),
        P("front", None, None, None),
    )
    out_specs = P("front", "row", "col")
    return jax.shard_map(
        per_device, mesh=mesh, in_specs=in_specs, out_specs=out_specs, check_vma=False
    )
```

```python
import jax
import jax.numpy as jnp
from jax import lax
from jax.experimental import pallas as pl
from jax.experimental.pallas import tpu as pltpu
from jax.sharding import PartitionSpec as P

PLANE = ("front", "row")
W = 256
SUBS = 4
FULL = SUBS * W
HALF = 2 * W
STRIP = 8
LANES = 128
NJ = 32
RING = 4
HBM = pl.BlockSpec(memory_space=pltpu.HBM)
VMEM = pl.BlockSpec(memory_space=pltpu.VMEM)
DMA = pltpu.SemaphoreType.DMA


def f32(*shape):
    return jax.ShapeDtypeStruct(shape, jnp.float32)


def space(*shape, dtype=jnp.float32):
    return pltpu.VMEM(shape, dtype)


def params(flops, moved, mib=18):
    return {
        "compiler_params": pltpu.CompilerParams(vmem_limit_bytes=mib * 1024 * 1024),
        "cost_estimate": pl.CostEstimate(flops=flops, bytes_accessed=moved, transcendentals=0),
    }


def split(value):
    high = value.astype(jnp.bfloat16)
    low = (value - high.astype(jnp.float32)).astype(jnp.bfloat16)
    return high, low


def dot(a, b):
    return jnp.dot(a, b, preferred_element_type=jnp.float32)


def dot3(a, b):
    ah, al = a
    bh, bl = b
    return dot(ah, bh) + (dot(ah, bl) + dot(al, bh))


def place_of(row, col):
    least = jnp.minimum(row, col)
    first = jnp.where(col == 0, row, 3 + col)
    second = jnp.where(col == 1, 6 + row, 8 + col)
    rest = 12 + (row - 2) * 2 + (col - 2)
    return jnp.where(least == 0, first, jnp.where(least == 1, second, rest))


PLACE = {}
for _r in range(SUBS):
    for _c in range(SUBS):
        PLACE[_r, _c] = (
            (_r if _c == 0 else 3 + _c)
            if min(_r, _c) == 0
            else (6 + _r if _c == 1 else 8 + _c)
            if min(_r, _c) == 1
            else 12 + (_r - 2) * 2 + _c - 2
        )


GROUPS = (4, 12, 12, 4)


def permute_kernel(
    dest_hbm, rows_hbm, cols_hbm, tiles_hbm, out_hbm, dest, rows, cols, tiles, out, sems, out_sems
):
    count = tiles.shape[0]
    maps = [
        pltpu.make_async_copy(rows_hbm, rows, sems.at[0]),
        pltpu.make_async_copy(cols_hbm, cols, sems.at[1]),
        pltpu.make_async_copy(dest_hbm, dest, sems.at[2]),
    ]
    loads = []
    first = 0
    for k, size in enumerate(GROUPS):
        at = pl.ds(first, size)
        loads.append(pltpu.make_async_copy(tiles_hbm.at[at], tiles.at[at], sems.at[3 + k]))
        first += size
    for copy in maps + loads:
        copy.start()
    for copy in maps:
        copy.wait()

    place = place_of(rows[:, :1] // W, cols[:, :1] // W).astype(jnp.float32)
    same = lax.broadcasted_iota(jnp.int32, (count, LANES), 0) == lax.broadcasted_iota(
        jnp.int32, (count, LANES), 1
    )
    line = jnp.sum(jnp.where(same, place, 0.0), axis=0, keepdims=True)
    out[:, 2 * count] = jnp.broadcast_to(line[None], (NJ, STRIP, LANES))
    line = line[:, :count] + (dest[...] * (SUBS * SUBS)).astype(jnp.float32)
    out[:, 2 * count, :, :count] = jnp.broadcast_to(line[None], (NJ, STRIP, count))

    index = lax.broadcasted_iota(jnp.int32, (W, W), 0)
    stores = []
    contract = (((1,), (1,)), ((), ()))
    first = 0
    for load, size in zip(loads, GROUPS):
        load.wait()
        for i in range(first, first + size):
            row_hot = (index == (rows[i : i + 1] & (W - 1))).astype(jnp.float32)
            col_hot = (index == (cols[i : i + 1] & (W - 1))).astype(jnp.float32)
            row_hot = row_hot.astype(jnp.bfloat16)
            col_hot = col_hot.astype(jnp.bfloat16)
            high, low = split(tiles[i])
            high = dot(row_hot, high).astype(jnp.bfloat16)
            low = dot(row_hot, low).astype(jnp.bfloat16)
            moved = lax.dot_general(
                jnp.concatenate([high, low], axis=1),
                jnp.concatenate([col_hot, col_hot], axis=1),
                contract,
                preferred_element_type=jnp.float32,
            )
            out[:, 2 * i] = moved[:, :LANES].reshape(NJ, STRIP, LANES)
            out[:, 2 * i + 1] = moved[:, LANES:].reshape(NJ, STRIP, LANES)
        at = pl.ds(2 * first, 2 * size + (first + size == count))
        sem = out_sems.at[len(stores)]
        stores.append(pltpu.make_async_copy(out.at[:, at], out_hbm.at[:, at], sem))
        stores[-1].start()
        first += size
    for store in stores:
        store.wait()


def permute_tiles(child_tiles, destination, row_map, col_map):
    count = child_tiles.shape[0]
    return pl.pallas_call(
        permute_kernel,
        in_specs=[HBM] * 4,
        out_specs=HBM,
        out_shape=f32(NJ, 2 * count + 1, STRIP, LANES),
        scratch_shapes=[
            space(1, count, dtype=jnp.int32),
            space(count, W, dtype=jnp.int32),
            space(count, W, dtype=jnp.int32),
            space(count, W, W),
            space(NJ, 2 * count + 1, STRIP, LANES),
            DMA((3 + len(GROUPS),)),
            DMA((len(GROUPS),)),
        ],
        name="permute",
        **params(8 * count * W**3, 8 * count * W * W, 62),
    )(destination.reshape(1, count), row_map, col_map, child_tiles)


def reduce_kernel(strips, sums, codes_vmem, codes, sem):
    count = strips.shape[1] // 2
    codes_vmem[...] = strips[:, 2 * count, 0].astype(jnp.int32)
    copy = pltpu.make_async_copy(codes_vmem, codes, sem)
    copy.start()
    sums[...] = jnp.zeros_like(sums)
    copy.wait()

    def add(source, carry):
        for k in range(count):
            code = codes[source, k]
            sums[code] = sums[code] + strips[source, 2 * k : 2 * k + 2]
        return carry

    lax.fori_loop(0, NJ, add, 0)


def reduce_strips(strips, slots):
    count = strips.shape[1] // 2
    return pl.pallas_call(
        reduce_kernel,
        in_specs=[VMEM],
        out_specs=VMEM,
        out_shape=f32(slots, 2, STRIP, LANES),
        scratch_shapes=[
            space(NJ, LANES, dtype=jnp.int32),
            pltpu.SMEM((NJ, LANES), jnp.int32),
            DMA,
        ],
        name="reduce",
        **params(NJ * count * STRIP * W, 4 * (NJ * count + slots) * STRIP * W),
    )(strips)


def block(parent, got, r, c):
    place = PLACE[r, c]
    rows, cols = slice(r * W, (r + 1) * W), c * W
    left = parent[rows, cols : cols + LANES] + got[:, place, 0].reshape(W, LANES)
    right = parent[rows, cols + LANES : cols + W] + got[:, place, 1].reshape(W, LANES)
    return jnp.concatenate([left, right], axis=1)


def first_kernel(parent, got, inv_ref, la, lb, ra, rb):
    inv = split(inv_ref[0])
    for k in range(SUBS):
        half = slice(k % 2 * W, (k % 2 + 1) * W)
        (la, lb)[k // 2][half] = dot3(split(block(parent, got, k, 0)), inv)
        (ra, rb)[k // 2][:, half] = block(parent, got, 0, k)


HALVES = [f32(HALF, W), f32(HALF, W), f32(W, HALF), f32(W, HALF)]


def first_panel(parent, got, inverses):
    return pl.pallas_call(
        first_kernel,
        in_specs=[VMEM] * 3,
        out_specs=[VMEM] * 4,
        out_shape=HALVES,
        name="first_panel",
        **params(6 * FULL * W * W, 12 * FULL * W),
    )(parent, got, inverses)


def assemble_kernel(parent, got, matrix):
    for r in range(SUBS):
        for c in range(SUBS):
            rows, cols = slice(r * W, (r + 1) * W), slice(c * W, (c + 1) * W)
            matrix[rows, cols] = block(parent, got, r, c)


def assemble(parent, got):
    return pl.pallas_call(
        assemble_kernel,
        in_specs=[VMEM] * 2,
        out_specs=VMEM,
        out_shape=f32(FULL, FULL),
        name="assemble",
        **params(FULL * FULL, 12 * FULL * FULL),
    )(parent, got)


def choose(index, near, parts, target):
    own, first, second = parts

    @pl.when(index == 0)
    def _():
        target[...] = own[...]

    @pl.when(index == near)
    def _():
        target[...] = first[...]

    @pl.when((index != 0) & (index != near))
    def _():
        target[...] = second[...]


def choose_all(row, col, pieces, left, right):
    choose(col, 1, pieces[0:3], left.at[pl.ds(0, HALF)])
    choose(col, 3, pieces[3:6], left.at[pl.ds(HALF, HALF)])
    choose(row, 1, pieces[6:9], right.at[:, pl.ds(0, HALF)])
    choose(row, 3, pieces[9:12], right.at[:, pl.ds(HALF, HALF)])


def second_kernel(*refs):
    pieces = refs[:12]
    matrix, inv_ref, la, lb, ra, rb, left, right = refs[12:]
    row, col = lax.axis_index("row"), lax.axis_index("col")

    @pl.when((row == 0) | (col == 0))
    def _():
        choose_all(row, col, pieces, left, right)

    @pl.when(col == 0)
    def _():
        inv = split(inv_ref[1])
        corner = split(right[:, W:HALF])
        for k in range(SUBS):
            at = slice(k * W, (k + 1) * W)
            half = slice(k % 2 * W, (k % 2 + 1) * W)
            reduced = matrix[at, W:HALF] - dot3(split(left[at]), corner)
            (la, lb)[k // 2][half] = dot3(split(reduced), inv)

    @pl.when(row == 0)
    def _():
        below = split(left[W:HALF])
        for k in range(SUBS):
            at = slice(k * W, (k + 1) * W)
            half = slice(k % 2 * W, (k % 2 + 1) * W)
            (ra, rb)[k // 2][:, half] = matrix[W:HALF, at] - dot3(below, split(right[:, at]))


def second_panel(pieces, matrix, inverses):
    return pl.pallas_call(
        second_kernel,
        in_specs=[VMEM] * 14,
        out_specs=[VMEM] * 4,
        out_shape=HALVES,
        scratch_shapes=[space(FULL, W), space(W, FULL)],
        name="second_panel",
        **params(18 * FULL * W * W, 32 * FULL * W),
    )(*pieces, matrix, inverses)


def update_rows(panel, k, matrix, out, left, high, low):
    row, col = lax.axis_index("row"), lax.axis_index("col")
    at = slice(k * W, (k + 1) * W)
    edge = (panel + 1) * W
    trailing = row * SUBS + k > panel
    values = left[at]
    factor = split(values)

    @pl.when(jnp.logical_not(trailing))
    def _():
        out[at] = matrix[at]

    @pl.when(trailing & (col == 0))
    def _():
        if panel:
            out[at, : panel * W] = matrix[at, : panel * W]
        out[at, panel * W : edge] = values
        out[at, edge:] = matrix[at, edge:] - dot3(factor, (high[:, edge:], low[:, edge:]))

    @pl.when(trailing & (col != 0))
    def _():
        out[at] = matrix[at] - dot3(factor, (high[...], low[...]))


def prepare(pieces, left, right, high, low):
    choose_all(lax.axis_index("row"), lax.axis_index("col"), pieces, left, right)
    values = split(right[...])
    high[...] = values[0]
    low[...] = values[1]


def update_kernel(*refs):
    matrix, out, left, right, high, low = refs[12:]
    prepare(refs[:12], left, right, high, low)
    for k in range(SUBS):
        update_rows(0, k, matrix, out, left, high, low)


def finish_kernel(*refs):
    matrix, out_hbm, left, right, high, low, out, sems = refs[12:]
    prepare(refs[:12], left, right, high, low)
    stores = []
    for k in range(SUBS):
        update_rows(1, k, matrix, out, left, high, low)
        at = pl.ds(k * W, W)
        stores.append(pltpu.make_async_copy(out.at[at], out_hbm.at[at], sems.at[k]))
        stores[k].start()
    for store in stores:
        store.wait()


SCRATCH = [
    space(FULL, W),
    space(W, FULL),
    space(W, FULL, dtype=jnp.bfloat16),
    space(W, FULL, dtype=jnp.bfloat16),
]


def update(matrix, pieces):
    return pl.pallas_call(
        update_kernel,
        in_specs=[VMEM] * 13,
        out_specs=VMEM,
        out_shape=f32(FULL, FULL),
        scratch_shapes=SCRATCH,
        name="update",
        **params(6 * FULL * FULL * W, 10 * FULL * FULL),
    )(*pieces, matrix)


def finish(matrix, pieces):
    return pl.pallas_call(
        finish_kernel,
        in_specs=[VMEM] * 13,
        out_specs=HBM,
        out_shape=f32(FULL, FULL),
        scratch_shapes=SCRATCH + [space(FULL, FULL), DMA((SUBS,))],
        name="finish",
        **params(6 * FULL * FULL * W, 10 * FULL * FULL),
    )(*pieces, matrix)


def exchange(value):
    return lax.all_to_all(value, PLANE, split_axis=0, concat_axis=0, tiled=True)


RIGHT = [(k, (k + 1) % RING) for k in range(RING)]
LEFT = [(k, (k - 1) % RING) for k in range(RING)]
PAIRS = [(0, 1), (1, 0), (2, 3), (3, 2)]
CROSS = [(0, 3), (3, 0), (1, 2), (2, 1)]


def pick_kernel(axis, near, own, got, out):
    index = lax.axis_index(axis)

    @pl.when(index == 0)
    def _():
        out[...] = own[...]

    @pl.when(index == near)
    def _():
        out[...] = got[...]


def pick(axis, near, own, got):
    return pl.pallas_call(
        lambda *refs: pick_kernel(axis, near, *refs),
        in_specs=[VMEM] * 2,
        out_specs=VMEM,
        out_shape=f32(*own.shape),
        name="pick",
        **params(0, 8 * HALF * W),
    )(own, got)


def broadcast(halves, beside=()):
    la, lb, ra, rb = halves
    la1 = lax.ppermute(la, "col", RIGHT)
    lb1 = lax.ppermute(lb, "col", LEFT)
    ra1 = lax.ppermute(ra, "row", RIGHT)
    rb1 = lax.ppermute(rb, "row", LEFT)
    la1, lb1 = lax.optimization_barrier((la1, lb1))
    ra1, rb1, beside = lax.optimization_barrier((ra1, rb1, beside))
    la2 = lax.ppermute(pick("col", 1, la, la1), "col", CROSS)
    ra2 = lax.ppermute(pick("row", 1, ra, ra1), "row", CROSS)
    lb2 = lax.ppermute(pick("col", 3, lb, lb1), "col", PAIRS)
    rb2 = lax.ppermute(pick("row", 3, rb, rb1), "row", PAIRS)
    return (la, la1, la2, lb, lb1, lb2, ra, ra1, ra2, rb, rb1, rb2), beside


def per_device(parent_front, child_tiles, destination, row_map, col_map, pivot_inverse):
    parent = parent_front[0]
    inverses = pivot_inverse[0]
    subs = SUBS * SUBS
    strips = exchange(permute_tiles(child_tiles, destination, row_map, col_map))
    got = exchange(reduce_strips(strips, NJ * subs).reshape(NJ, subs, 2, STRIP, LANES))
    pieces, matrix = broadcast(first_panel(parent, got, inverses), assemble(parent, got))
    second = second_panel(pieces, matrix, inverses)
    later, matrix = broadcast(second, update(matrix, pieces))
    return finish(matrix, later)[None]


def solution(mesh):
    in_specs = (
        P("front", "row", "col"),
        P(("front", "row", "col"), None, None),
        P(("front", "row", "col"), None),
        P(("front", "row", "col"), None),
        P(("front", "row", "col"), None),
        P("front", None, None, None),
    )
    out_specs = P("front", "row", "col")
    return jax.shard_map(
        per_device, mesh=mesh, in_specs=in_specs, out_specs=out_specs, check_vma=False
    )
```

```python
import jax
import jax.numpy as jnp
from jax import lax
from jax.experimental import pallas as pl
from jax.experimental.pallas import tpu as pltpu
from jax.sharding import PartitionSpec as P

PLANE = ("front", "row")
W = 256
SUBS = 4
FULL = SUBS * W
HALF = 2 * W
STRIP = 8
LANES = 128
NJ = 32
RING = 4
HBM = pl.BlockSpec(memory_space=pltpu.HBM)
VMEM = pl.BlockSpec(memory_space=pltpu.VMEM)
DMA = pltpu.SemaphoreType.DMA


def f32(*shape):
    return jax.ShapeDtypeStruct(shape, jnp.float32)


def space(*shape, dtype=jnp.float32):
    return pltpu.VMEM(shape, dtype)


def params(flops, moved, mib=18):
    return {
        "compiler_params": pltpu.CompilerParams(vmem_limit_bytes=mib * 1024 * 1024),
        "cost_estimate": pl.CostEstimate(flops=flops, bytes_accessed=moved, transcendentals=0),
    }


def split(value):
    high = value.astype(jnp.bfloat16)
    low = (value - high.astype(jnp.float32)).astype(jnp.bfloat16)
    return high, low


def dot(a, b):
    return jnp.dot(a, b, preferred_element_type=jnp.float32)


def dot3(a, b):
    ah, al = a
    bh, bl = b
    return dot(ah, bh) + (dot(ah, bl) + dot(al, bh))


def place_of(row, col):
    least = jnp.minimum(row, col)
    first = jnp.where(col == 0, row, 3 + col)
    second = jnp.where(col == 1, 6 + row, 8 + col)
    rest = 12 + (row - 2) * 2 + (col - 2)
    return jnp.where(least == 0, first, jnp.where(least == 1, second, rest))


PLACE = {}
for _r in range(SUBS):
    for _c in range(SUBS):
        PLACE[_r, _c] = (
            (_r if _c == 0 else 3 + _c)
            if min(_r, _c) == 0
            else (6 + _r if _c == 1 else 8 + _c)
            if min(_r, _c) == 1
            else 12 + (_r - 2) * 2 + _c - 2
        )


GROUPS = (4, 12, 12, 4)


def permute_kernel(
    dest_hbm, rows_hbm, cols_hbm, tiles_hbm, out_hbm, dest, rows, cols, tiles, out, sems, out_sems
):
    count = tiles.shape[0]
    maps = [
        pltpu.make_async_copy(rows_hbm, rows, sems.at[0]),
        pltpu.make_async_copy(cols_hbm, cols, sems.at[1]),
        pltpu.make_async_copy(dest_hbm, dest, sems.at[2]),
    ]
    loads = []
    first = 0
    for k, size in enumerate(GROUPS):
        at = pl.ds(first, size)
        loads.append(pltpu.make_async_copy(tiles_hbm.at[at], tiles.at[at], sems.at[3 + k]))
        first += size
    for copy in maps + loads:
        copy.start()
    for copy in maps:
        copy.wait()

    place = place_of(rows[:, :1] // W, cols[:, :1] // W).astype(jnp.float32)
    same = lax.broadcasted_iota(jnp.int32, (count, LANES), 0) == lax.broadcasted_iota(
        jnp.int32, (count, LANES), 1
    )
    line = jnp.sum(jnp.where(same, place, 0.0), axis=0, keepdims=True)
    out[:, 2 * count] = jnp.broadcast_to(line[None], (NJ, STRIP, LANES))
    line = line[:, :count] + (dest[...] * (SUBS * SUBS)).astype(jnp.float32)
    out[:, 2 * count, :, :count] = jnp.broadcast_to(line[None], (NJ, STRIP, count))

    index = lax.broadcasted_iota(jnp.int32, (W, W), 0)
    stores = []
    contract = (((1,), (1,)), ((), ()))
    first = 0
    for load, size in zip(loads, GROUPS):
        load.wait()
        for i in range(first, first + size):
            row_hot = (index == (rows[i : i + 1] & (W - 1))).astype(jnp.float32)
            col_hot = (index == (cols[i : i + 1] & (W - 1))).astype(jnp.float32)
            row_hot = row_hot.astype(jnp.bfloat16)
            col_hot = col_hot.astype(jnp.bfloat16)
            high, low = split(tiles[i])
            high = dot(row_hot, high).astype(jnp.bfloat16)
            low = dot(row_hot, low).astype(jnp.bfloat16)
            moved = lax.dot_general(
                jnp.concatenate([high, low], axis=1),
                jnp.concatenate([col_hot, col_hot], axis=1),
                contract,
                preferred_element_type=jnp.float32,
            )
            out[:, 2 * i] = moved[:, :LANES].reshape(NJ, STRIP, LANES)
            out[:, 2 * i + 1] = moved[:, LANES:].reshape(NJ, STRIP, LANES)
        at = pl.ds(2 * first, 2 * size + (first + size == count))
        sem = out_sems.at[len(stores)]
        stores.append(pltpu.make_async_copy(out.at[:, at], out_hbm.at[:, at], sem))
        stores[-1].start()
        first += size
    for store in stores:
        store.wait()


def permute_tiles(child_tiles, destination, row_map, col_map):
    count = child_tiles.shape[0]
    return pl.pallas_call(
        permute_kernel,
        in_specs=[HBM] * 4,
        out_specs=HBM,
        out_shape=f32(NJ, 2 * count + 1, STRIP, LANES),
        scratch_shapes=[
            space(1, count, dtype=jnp.int32),
            space(count, W, dtype=jnp.int32),
            space(count, W, dtype=jnp.int32),
            space(count, W, W),
            space(NJ, 2 * count + 1, STRIP, LANES),
            DMA((3 + len(GROUPS),)),
            DMA((len(GROUPS),)),
        ],
        name="permute",
        **params(8 * count * W**3, 8 * count * W * W, 62),
    )(destination.reshape(1, count), row_map, col_map, child_tiles)


def reduce_kernel(strips, sums, codes_vmem, codes, sem):
    count = strips.shape[1] // 2
    codes_vmem[...] = strips[:, 2 * count, 0].astype(jnp.int32)
    copy = pltpu.make_async_copy(codes_vmem, codes, sem)
    copy.start()
    sums[...] = jnp.zeros_like(sums)
    copy.wait()

    def add(source, carry):
        for k in range(count):
            code = codes[source, k]
            sums[code] = sums[code] + strips[source, 2 * k : 2 * k + 2]
        return carry

    lax.fori_loop(0, NJ, add, 0)


def reduce_strips(strips, slots):
    count = strips.shape[1] // 2
    return pl.pallas_call(
        reduce_kernel,
        in_specs=[VMEM],
        out_specs=VMEM,
        out_shape=f32(slots, 2, STRIP, LANES),
        scratch_shapes=[
            space(NJ, LANES, dtype=jnp.int32),
            pltpu.SMEM((NJ, LANES), jnp.int32),
            DMA,
        ],
        name="reduce",
        **params(NJ * count * STRIP * W, 4 * (NJ * count + slots) * STRIP * W),
    )(strips)


def block(parent, got, r, c):
    place = PLACE[r, c]
    rows, cols = slice(r * W, (r + 1) * W), c * W
    left = parent[rows, cols : cols + LANES] + got[:, place, 0].reshape(W, LANES)
    right = parent[rows, cols + LANES : cols + W] + got[:, place, 1].reshape(W, LANES)
    return jnp.concatenate([left, right], axis=1)


def first_kernel(parent, got, inv_ref, la, lb, ra, rb):
    inv = split(inv_ref[0])
    for k in range(SUBS):
        half = slice(k % 2 * W, (k % 2 + 1) * W)
        (la, lb)[k // 2][half] = dot3(split(block(parent, got, k, 0)), inv)
        (ra, rb)[k // 2][:, half] = block(parent, got, 0, k)


HALVES = [f32(HALF, W), f32(HALF, W), f32(W, HALF), f32(W, HALF)]


def first_panel(parent, got, inverses):
    return pl.pallas_call(
        first_kernel,
        in_specs=[VMEM] * 3,
        out_specs=[VMEM] * 4,
        out_shape=HALVES,
        name="first_panel",
        **params(6 * FULL * W * W, 12 * FULL * W),
    )(parent, got, inverses)


def assemble_kernel(parent, got, matrix):
    for r in range(SUBS):
        for c in range(SUBS):
            rows, cols = slice(r * W, (r + 1) * W), slice(c * W, (c + 1) * W)
            matrix[rows, cols] = block(parent, got, r, c)


def assemble(parent, got):
    return pl.pallas_call(
        assemble_kernel,
        in_specs=[VMEM] * 2,
        out_specs=VMEM,
        out_shape=f32(FULL, FULL),
        name="assemble",
        **params(FULL * FULL, 12 * FULL * FULL),
    )(parent, got)


def choose(index, near, parts, target):
    own, first, second = parts

    @pl.when(index == 0)
    def _():
        target[...] = own[...]

    @pl.when(index == near)
    def _():
        target[...] = first[...]

    @pl.when((index != 0) & (index != near))
    def _():
        target[...] = second[...]


def choose_all(row, col, pieces, left, right):
    choose(col, 1, pieces[0:3], left.at[pl.ds(0, HALF)])
    choose(col, 3, pieces[3:6], left.at[pl.ds(HALF, HALF)])
    choose(row, 1, pieces[6:9], right.at[:, pl.ds(0, HALF)])
    choose(row, 3, pieces[9:12], right.at[:, pl.ds(HALF, HALF)])


def second_kernel(*refs):
    pieces = refs[:12]
    matrix, inv_ref, la, lb, ra, rb, left, right = refs[12:]
    row, col = lax.axis_index("row"), lax.axis_index("col")

    @pl.when((row == 0) | (col == 0))
    def _():
        choose_all(row, col, pieces, left, right)

    @pl.when(col == 0)
    def _():
        inv = split(inv_ref[1])
        corner = split(right[:, W:HALF])
        for k in range(SUBS):
            at = slice(k * W, (k + 1) * W)
            half = slice(k % 2 * W, (k % 2 + 1) * W)
            reduced = matrix[at, W:HALF] - dot3(split(left[at]), corner)
            (la, lb)[k // 2][half] = dot3(split(reduced), inv)

    @pl.when(row == 0)
    def _():
        below = split(left[W:HALF])
        for k in range(SUBS):
            at = slice(k * W, (k + 1) * W)
            half = slice(k % 2 * W, (k % 2 + 1) * W)
            (ra, rb)[k // 2][:, half] = matrix[W:HALF, at] - dot3(below, split(right[:, at]))


def second_panel(pieces, matrix, inverses):
    return pl.pallas_call(
        second_kernel,
        in_specs=[VMEM] * 14,
        out_specs=[VMEM] * 4,
        out_shape=HALVES,
        scratch_shapes=[space(FULL, W), space(W, FULL)],
        name="second_panel",
        **params(18 * FULL * W * W, 32 * FULL * W),
    )(*pieces, matrix, inverses)


def update_rows(panel, k, matrix, out, left, high, low):
    row, col = lax.axis_index("row"), lax.axis_index("col")
    at = slice(k * W, (k + 1) * W)
    edge = (panel + 1) * W
    trailing = row * SUBS + k > panel
    values = left[at]
    factor = split(values)

    @pl.when(jnp.logical_not(trailing))
    def _():
        out[at] = matrix[at]

    @pl.when(trailing & (col == 0))
    def _():
        if panel:
            out[at, : panel * W] = matrix[at, : panel * W]
        out[at, panel * W : edge] = values
        out[at, edge:] = matrix[at, edge:] - dot3(factor, (high[:, edge:], low[:, edge:]))

    @pl.when(trailing & (col != 0))
    def _():
        out[at] = matrix[at] - dot3(factor, (high[...], low[...]))


def prepare(pieces, left, right, high, low):
    choose_all(lax.axis_index("row"), lax.axis_index("col"), pieces, left, right)
    values = split(right[...])
    high[...] = values[0]
    low[...] = values[1]


def update_kernel(*refs):
    matrix, out, left, right, high, low = refs[12:]
    prepare(refs[:12], left, right, high, low)
    for k in range(SUBS):
        update_rows(0, k, matrix, out, left, high, low)


def finish_kernel(*refs):
    matrix, out_hbm, left, right, high, low, out, sems = refs[12:]
    prepare(refs[:12], left, right, high, low)
    stores = []
    for k in range(SUBS):
        update_rows(1, k, matrix, out, left, high, low)
        at = pl.ds(k * W, W)
        stores.append(pltpu.make_async_copy(out.at[at], out_hbm.at[at], sems.at[k]))
        stores[k].start()
    for store in stores:
        store.wait()


SCRATCH = [
    space(FULL, W),
    space(W, FULL),
    space(W, FULL, dtype=jnp.bfloat16),
    space(W, FULL, dtype=jnp.bfloat16),
]


def update(matrix, pieces):
    return pl.pallas_call(
        update_kernel,
        in_specs=[VMEM] * 13,
        out_specs=VMEM,
        out_shape=f32(FULL, FULL),
        scratch_shapes=SCRATCH,
        name="update",
        **params(6 * FULL * FULL * W, 10 * FULL * FULL),
    )(*pieces, matrix)


def finish(matrix, pieces):
    return pl.pallas_call(
        finish_kernel,
        in_specs=[VMEM] * 13,
        out_specs=HBM,
        out_shape=f32(FULL, FULL),
        scratch_shapes=SCRATCH + [space(FULL, FULL), DMA((SUBS,))],
        name="finish",
        **params(6 * FULL * FULL * W, 10 * FULL * FULL),
    )(*pieces, matrix)


def exchange(value):
    return lax.all_to_all(value, PLANE, split_axis=0, concat_axis=0, tiled=True)


PAIRS = [(0, 1), (1, 0), (2, 3), (3, 2)]
CROSS = [(0, 3), (3, 0), (1, 2), (2, 1)]


def pick_kernel(axis, near, own, got, out):
    index = lax.axis_index(axis)

    @pl.when(index == 0)
    def _():
        out[...] = own[...]

    @pl.when(index == near)
    def _():
        out[...] = got[...]


def pick(axis, near, own, got):
    return pl.pallas_call(
        lambda *refs: pick_kernel(axis, near, *refs),
        in_specs=[VMEM] * 2,
        out_specs=VMEM,
        out_shape=f32(*own.shape),
        name="pick",
        **params(0, 8 * HALF * W),
    )(own, got)


def broadcast(halves, beside=()):
    la, lb, ra, rb = halves
    la1 = lax.ppermute(la, "col", PAIRS)
    lb1 = lax.ppermute(lb, "col", CROSS)
    ra1 = lax.ppermute(ra, "row", PAIRS)
    rb1 = lax.ppermute(rb, "row", CROSS)
    la1, lb1 = lax.optimization_barrier((la1, lb1))
    ra1, rb1, beside = lax.optimization_barrier((ra1, rb1, beside))
    la2 = lax.ppermute(pick("col", 1, la, la1), "col", CROSS)
    ra2 = lax.ppermute(pick("row", 1, ra, ra1), "row", CROSS)
    lb2 = lax.ppermute(pick("col", 3, lb, lb1), "col", PAIRS)
    rb2 = lax.ppermute(pick("row", 3, rb, rb1), "row", PAIRS)
    return (la, la1, la2, lb, lb1, lb2, ra, ra1, ra2, rb, rb1, rb2), beside


def per_device(parent_front, child_tiles, destination, row_map, col_map, pivot_inverse):
    parent = parent_front[0]
    inverses = pivot_inverse[0]
    subs = SUBS * SUBS
    strips = exchange(permute_tiles(child_tiles, destination, row_map, col_map))
    got = exchange(reduce_strips(strips, NJ * subs).reshape(NJ, subs, 2, STRIP, LANES))
    pieces, matrix = broadcast(first_panel(parent, got, inverses), assemble(parent, got))
    second = second_panel(pieces, matrix, inverses)
    later, matrix = broadcast(second, update(matrix, pieces))
    return finish(matrix, later)[None]


def solution(mesh):
    in_specs = (
        P("front", "row", "col"),
        P(("front", "row", "col"), None, None),
        P(("front", "row", "col"), None),
        P(("front", "row", "col"), None),
        P(("front", "row", "col"), None),
        P("front", None, None, None),
    )
    out_specs = P("front", "row", "col")
    return jax.shard_map(
        per_device, mesh=mesh, in_specs=in_specs, out_specs=out_specs, check_vma=False
    )
```

```python
import jax
import jax.numpy as jnp
from jax import lax
from jax.experimental import pallas as pl
from jax.experimental.pallas import tpu as pltpu
from jax.sharding import PartitionSpec as P

PLANE = ("front", "row")
W = 256
SUBS = 4
FULL = SUBS * W
HALF = 2 * W
STRIP = 8
LANES = 128
NJ = 32
ANY = pl.BlockSpec(memory_space=pl.ANY)
HBM = pl.BlockSpec(memory_space=pltpu.HBM)
VMEM = pl.BlockSpec(memory_space=pltpu.VMEM)
DMA = pltpu.SemaphoreType.DMA


def f32(*shape):
    return jax.ShapeDtypeStruct(shape, jnp.float32)


def space(*shape, dtype=jnp.float32):
    return pltpu.VMEM(shape, dtype)


def params(flops, moved, mib=18):
    return {
        "compiler_params": pltpu.CompilerParams(vmem_limit_bytes=mib * 1024 * 1024),
        "cost_estimate": pl.CostEstimate(flops=flops, bytes_accessed=moved, transcendentals=0),
    }


def split(value):
    high = value.astype(jnp.bfloat16)
    low = (value - high.astype(jnp.float32)).astype(jnp.bfloat16)
    return high, low


def dot(a, b):
    return jnp.dot(a, b, preferred_element_type=jnp.float32)


def dot3(a, b):
    ah, al = a
    bh, bl = b
    return dot(ah, bh) + (dot(ah, bl) + dot(al, bh))


def place_of(row, col):
    least = jnp.minimum(row, col)
    first = jnp.where(col == 0, row, 3 + col)
    second = jnp.where(col == 1, 6 + row, 8 + col)
    rest = 12 + (row - 2) * 2 + (col - 2)
    return jnp.where(least == 0, first, jnp.where(least == 1, second, rest))


PLACE = {}
for _r in range(SUBS):
    for _c in range(SUBS):
        PLACE[_r, _c] = (
            (_r if _c == 0 else 3 + _c)
            if min(_r, _c) == 0
            else (6 + _r if _c == 1 else 8 + _c)
            if min(_r, _c) == 1
            else 12 + (_r - 2) * 2 + _c - 2
        )


GROUPS = (4, 12, 12, 4)


def permute_kernel(
    dest_hbm, rows_hbm, cols_hbm, tiles_hbm, out_hbm, dest, rows, cols, tiles, out, sems, out_sems
):
    count = tiles.shape[0]
    maps = [
        pltpu.make_async_copy(rows_hbm, rows, sems.at[0]),
        pltpu.make_async_copy(cols_hbm, cols, sems.at[1]),
        pltpu.make_async_copy(dest_hbm, dest, sems.at[2]),
    ]
    loads = []
    first = 0
    for k, size in enumerate(GROUPS):
        at = pl.ds(first, size)
        loads.append(pltpu.make_async_copy(tiles_hbm.at[at], tiles.at[at], sems.at[3 + k]))
        first += size
    for copy in maps + loads:
        copy.start()
    for copy in maps:
        copy.wait()

    place = place_of(rows[:, :1] // W, cols[:, :1] // W).astype(jnp.float32)
    same = lax.broadcasted_iota(jnp.int32, (count, LANES), 0) == lax.broadcasted_iota(
        jnp.int32, (count, LANES), 1
    )
    line = jnp.sum(jnp.where(same, place, 0.0), axis=0, keepdims=True)
    out[:, 2 * count] = jnp.broadcast_to(line[None], (NJ, STRIP, LANES))
    line = line[:, :count] + (dest[...] * (SUBS * SUBS)).astype(jnp.float32)
    out[:, 2 * count, :, :count] = jnp.broadcast_to(line[None], (NJ, STRIP, count))

    index = lax.broadcasted_iota(jnp.int32, (W, W), 0)
    stores = []
    contract = (((1,), (1,)), ((), ()))
    first = 0
    for load, size in zip(loads, GROUPS):
        load.wait()
        for i in range(first, first + size):
            row_hot = (index == (rows[i : i + 1] & (W - 1))).astype(jnp.float32)
            col_hot = (index == (cols[i : i + 1] & (W - 1))).astype(jnp.float32)
            row_hot = row_hot.astype(jnp.bfloat16)
            col_hot = col_hot.astype(jnp.bfloat16)
            high, low = split(tiles[i])
            high = dot(row_hot, high).astype(jnp.bfloat16)
            low = dot(row_hot, low).astype(jnp.bfloat16)
            moved = lax.dot_general(
                jnp.concatenate([high, low], axis=1),
                jnp.concatenate([col_hot, col_hot], axis=1),
                contract,
                preferred_element_type=jnp.float32,
            )
            out[:, 2 * i] = moved[:, :LANES].reshape(NJ, STRIP, LANES)
            out[:, 2 * i + 1] = moved[:, LANES:].reshape(NJ, STRIP, LANES)
        at = pl.ds(2 * first, 2 * size + (first + size == count))
        sem = out_sems.at[len(stores)]
        stores.append(pltpu.make_async_copy(out.at[:, at], out_hbm.at[:, at], sem))
        stores[-1].start()
        first += size
    for store in stores:
        store.wait()


def permute_tiles(child_tiles, destination, row_map, col_map):
    count = child_tiles.shape[0]
    return pl.pallas_call(
        permute_kernel,
        in_specs=[HBM] * 4,
        out_specs=HBM,
        out_shape=f32(NJ, 2 * count + 1, STRIP, LANES),
        scratch_shapes=[
            space(1, count, dtype=jnp.int32),
            space(count, W, dtype=jnp.int32),
            space(count, W, dtype=jnp.int32),
            space(count, W, W),
            space(NJ, 2 * count + 1, STRIP, LANES),
            DMA((3 + len(GROUPS),)),
            DMA((len(GROUPS),)),
        ],
        name="permute",
        **params(8 * count * W**3, 8 * count * W * W, 62),
    )(destination.reshape(1, count), row_map, col_map, child_tiles)


def reduce_kernel(strips, sums, codes_vmem, codes, sem):
    count = strips.shape[1] // 2
    codes_vmem[...] = strips[:, 2 * count, 0].astype(jnp.int32)
    copy = pltpu.make_async_copy(codes_vmem, codes, sem)
    copy.start()
    sums[...] = jnp.zeros_like(sums)
    copy.wait()

    def add(source, carry):
        for k in range(count):
            code = codes[source, k]
            sums[code] = sums[code] + strips[source, 2 * k : 2 * k + 2]
        return carry

    lax.fori_loop(0, NJ, add, 0)


def reduce_strips(strips, slots):
    count = strips.shape[1] // 2
    return pl.pallas_call(
        reduce_kernel,
        in_specs=[VMEM],
        out_specs=VMEM,
        out_shape=f32(slots, 2, STRIP, LANES),
        scratch_shapes=[
            space(NJ, LANES, dtype=jnp.int32),
            pltpu.SMEM((NJ, LANES), jnp.int32),
            DMA,
        ],
        name="reduce",
        **params(NJ * count * STRIP * W, 4 * (NJ * count + slots) * STRIP * W),
    )(strips)


def block(parent, got, r, c):
    place = PLACE[r, c]
    rows, cols = slice(r * W, (r + 1) * W), c * W
    left = parent[rows, cols : cols + LANES] + got[:, place, 0].reshape(W, LANES)
    right = parent[rows, cols + LANES : cols + W] + got[:, place, 1].reshape(W, LANES)
    return jnp.concatenate([left, right], axis=1)


def first_factor_kernel(parent, got, inv_ref, la, lb):
    inv = split(inv_ref[0])
    for k in range(SUBS):
        half = slice(k % 2 * W, (k % 2 + 1) * W)
        (la, lb)[k // 2][half] = dot3(split(block(parent, got, k, 0)), inv)


def first_factor(parent, got, inverses):
    return pl.pallas_call(
        first_factor_kernel,
        in_specs=[VMEM] * 3,
        out_specs=[VMEM] * 2,
        out_shape=[f32(HALF, W)] * 2,
        name="first_factor",
        **params(6 * FULL * W * W, 12 * FULL * W),
    )(parent, got, inverses)


def first_rows_kernel(parent, got, after, ra, rb):
    for k in range(SUBS):
        (ra, rb)[k // 2][:, k % 2 * W : (k % 2 + 1) * W] = block(parent, got, 0, k)


def first_rows(parent, got, after):
    return pl.pallas_call(
        first_rows_kernel,
        in_specs=[VMEM] * 2 + [ANY],
        out_specs=[VMEM] * 2,
        out_shape=[f32(W, HALF)] * 2,
        name="first_rows",
        **params(FULL * W, 12 * FULL * W),
    )(parent, got, after)


def assemble_kernel(parent, got, matrix):
    for r in range(SUBS):
        for c in range(SUBS):
            rows, cols = slice(r * W, (r + 1) * W), slice(c * W, (c + 1) * W)
            matrix[rows, cols] = block(parent, got, r, c)


def assemble(parent, got):
    return pl.pallas_call(
        assemble_kernel,
        in_specs=[VMEM] * 2,
        out_specs=VMEM,
        out_shape=f32(FULL, FULL),
        name="assemble",
        **params(FULL * FULL, 12 * FULL * FULL),
    )(parent, got)


def choose(index, near, parts, target):
    own, first, second = parts

    @pl.when(index == 0)
    def _():
        target[...] = own[...]

    @pl.when(index == near)
    def _():
        target[...] = first[...]

    @pl.when((index != 0) & (index != near))
    def _():
        target[...] = second[...]


def choose_all(row, col, pieces, left, right):
    choose(col, 1, pieces[0:3], left.at[pl.ds(0, HALF)])
    choose(col, 3, pieces[3:6], left.at[pl.ds(HALF, HALF)])
    choose(row, 1, pieces[6:9], right.at[:, pl.ds(0, HALF)])
    choose(row, 3, pieces[9:12], right.at[:, pl.ds(HALF, HALF)])


def second_factor_kernel(*refs):
    pieces = refs[:9]
    matrix, inv_ref, la, lb, right = refs[9:]

    @pl.when(lax.axis_index("col") == 0)
    def _():
        choose(lax.axis_index("row"), 1, pieces[6:9], right)
        inv = split(inv_ref[1])
        corner = split(right[:, W:])
        for k in range(SUBS):
            at = slice(k * W, (k + 1) * W)
            half = slice(k % 2 * W, (k % 2 + 1) * W)
            reduced = matrix[at, W:HALF] - dot3(split(pieces[3 * (k // 2)][half]), corner)
            (la, lb)[k // 2][half] = dot3(split(reduced), inv)


def second_factor(pieces, matrix, inverses):
    return pl.pallas_call(
        second_factor_kernel,
        in_specs=[VMEM] * 11,
        out_specs=[VMEM] * 2,
        out_shape=[f32(HALF, W)] * 2,
        scratch_shapes=[space(W, HALF)],
        name="second_factor",
        **params(12 * FULL * W * W, 16 * FULL * W),
    )(*pieces[:9], matrix, inverses)


def second_rows_kernel(*refs):
    pieces = refs[:9]
    matrix, after, ra, rb, left = refs[9:]

    @pl.when(lax.axis_index("row") == 0)
    def _():
        choose(lax.axis_index("col"), 1, pieces[0:3], left)
        below = split(left[W:])
        for k in range(SUBS):
            at = slice(k * W, (k + 1) * W)
            half = slice(k % 2 * W, (k % 2 + 1) * W)
            pivot = split(pieces[3 + 3 * (k // 2)][:, half])
            (ra, rb)[k // 2][:, half] = matrix[W:HALF, at] - dot3(below, pivot)


def second_rows(pieces, matrix, after):
    return pl.pallas_call(
        second_rows_kernel,
        in_specs=[VMEM] * 10 + [ANY],
        out_specs=[VMEM] * 2,
        out_shape=[f32(W, HALF)] * 2,
        scratch_shapes=[space(HALF, W)],
        name="second_rows",
        **params(6 * FULL * W * W, 16 * FULL * W),
    )(*pieces[:3], *pieces[6:12], matrix, after)


def update_rows(panel, k, matrix, out, left, high, low):
    row, col = lax.axis_index("row"), lax.axis_index("col")
    at = slice(k * W, (k + 1) * W)
    edge = (panel + 1) * W
    trailing = row * SUBS + k > panel
    values = left[at]
    factor = split(values)

    @pl.when(jnp.logical_not(trailing))
    def _():
        out[at] = matrix[at]

    @pl.when(trailing & (col == 0))
    def _():
        if panel:
            out[at, : panel * W] = matrix[at, : panel * W]
        out[at, panel * W : edge] = values
        out[at, edge:] = matrix[at, edge:] - dot3(factor, (high[:, edge:], low[:, edge:]))

    @pl.when(trailing & (col != 0))
    def _():
        out[at] = matrix[at] - dot3(factor, (high[...], low[...]))


def prepare(pieces, left, right, high, low):
    choose_all(lax.axis_index("row"), lax.axis_index("col"), pieces, left, right)
    values = split(right[...])
    high[...] = values[0]
    low[...] = values[1]


def update_kernel(*refs):
    matrix, out, left, right, high, low = refs[12:]
    prepare(refs[:12], left, right, high, low)
    for k in range(SUBS):
        update_rows(0, k, matrix, out, left, high, low)


def finish_kernel(*refs):
    matrix, out_hbm, left, right, high, low, out, sems = refs[12:]
    prepare(refs[:12], left, right, high, low)
    stores = []
    for k in range(SUBS):
        update_rows(1, k, matrix, out, left, high, low)
        at = pl.ds(k * W, W)
        stores.append(pltpu.make_async_copy(out.at[at], out_hbm.at[at], sems.at[k]))
        stores[k].start()
    for store in stores:
        store.wait()


SCRATCH = [
    space(FULL, W),
    space(W, FULL),
    space(W, FULL, dtype=jnp.bfloat16),
    space(W, FULL, dtype=jnp.bfloat16),
]


def update(matrix, pieces):
    return pl.pallas_call(
        update_kernel,
        in_specs=[VMEM] * 13,
        out_specs=VMEM,
        out_shape=f32(FULL, FULL),
        scratch_shapes=SCRATCH,
        name="update",
        **params(6 * FULL * FULL * W, 10 * FULL * FULL),
    )(*pieces, matrix)


def finish(matrix, pieces):
    return pl.pallas_call(
        finish_kernel,
        in_specs=[VMEM] * 13,
        out_specs=HBM,
        out_shape=f32(FULL, FULL),
        scratch_shapes=SCRATCH + [space(FULL, FULL), DMA((SUBS,))],
        name="finish",
        **params(6 * FULL * FULL * W, 10 * FULL * FULL),
    )(*pieces, matrix)


def exchange(value):
    return lax.all_to_all(value, PLANE, split_axis=0, concat_axis=0, tiled=True)


PAIRS = [(0, 1), (1, 0), (2, 3), (3, 2)]
CROSS = [(0, 3), (3, 0), (1, 2), (2, 1)]


def pick_kernel(axis, near, own, got, out):
    index = lax.axis_index(axis)

    @pl.when(index == 0)
    def _():
        out[...] = own[...]

    @pl.when(index == near)
    def _():
        out[...] = got[...]


def pick(axis, near, own, got):
    return pl.pallas_call(
        lambda *refs: pick_kernel(axis, near, *refs),
        in_specs=[VMEM] * 2,
        out_specs=VMEM,
        out_shape=f32(*own.shape),
        name="pick",
        **params(0, 8 * HALF * W),
    )(own, got)


def broadcast(halves, beside=()):
    la, lb, ra, rb = halves
    la1 = lax.ppermute(la, "col", PAIRS)
    lb1 = lax.ppermute(lb, "col", CROSS)
    ra1 = lax.ppermute(ra, "row", PAIRS)
    rb1 = lax.ppermute(rb, "row", CROSS)
    la1, lb1 = lax.optimization_barrier((la1, lb1))
    ra1, rb1, beside = lax.optimization_barrier((ra1, rb1, beside))
    la2 = lax.ppermute(pick("col", 1, la, la1), "col", CROSS)
    ra2 = lax.ppermute(pick("row", 1, ra, ra1), "row", CROSS)
    lb2 = lax.ppermute(pick("col", 3, lb, lb1), "col", PAIRS)
    rb2 = lax.ppermute(pick("row", 3, rb, rb1), "row", PAIRS)
    return (la, la1, la2, lb, lb1, lb2, ra, ra1, ra2, rb, rb1, rb2), beside


def per_device(parent_front, child_tiles, destination, row_map, col_map, pivot_inverse):
    parent = parent_front[0]
    inverses = pivot_inverse[0]
    subs = SUBS * SUBS
    strips = exchange(permute_tiles(child_tiles, destination, row_map, col_map))
    got = exchange(reduce_strips(strips, NJ * subs).reshape(NJ, subs, 2, STRIP, LANES))
    la, lb = first_factor(parent, got, inverses)
    ra, rb = first_rows(parent, got, la)
    pieces, matrix = broadcast((la, lb, ra, rb), assemble(parent, got))
    la, lb = second_factor(pieces, matrix, inverses)
    ra, rb = second_rows(pieces, matrix, la)
    later, matrix = broadcast((la, lb, ra, rb), update(matrix, pieces))
    return finish(matrix, later)[None]


def solution(mesh):
    in_specs = (
        P("front", "row", "col"),
        P(("front", "row", "col"), None, None),
        P(("front", "row", "col"), None),
        P(("front", "row", "col"), None),
        P(("front", "row", "col"), None),
        P("front", None, None, None),
    )
    out_specs = P("front", "row", "col")
    return jax.shard_map(
        per_device, mesh=mesh, in_specs=in_specs, out_specs=out_specs, check_vma=False
    )
```
